32 devices in a mesh: groups: 2 (over y), ctx: 16 (over z, x, core).
Axes of the slice: x: 2, y: 2, z: 4, core: 2. Of those that a mesh axis runs over, the one named last changes fastest.
Arguments:
- queries: bfloat16 [12288, 1024], P(('groups', 'ctx')), parts along dimension 0, may hold values from -6 to 6
- keys: bfloat16 [12288, 1024], P(('groups', 'ctx')), parts along dimension 0, may hold values from -6 to 6
- values: bfloat16 [12288, 1024], P(('groups', 'ctx')), parts along dimension 0, may hold values from -6 to 6
- reset_points: int32 [16], P('groups'), parts along dimension 0, may hold values from 1 to 6143, as said below
- norm_gain: float32 [1024], replicated, may hold values from 0.1 to 1.9
- out_weight: bfloat16 [1024, 2048], P(None, 'ctx'), may hold values from -0.1875 to 0.1875
Outputs:
- attended: bfloat16 [12288, 2048], P(('groups', 'ctx')), parts along dimension 0
The draws below stay inside these ranges and needn't reach their ends.
There are 2 independent parts, one for each index of `groups`. The reference program is written for one: setup_inputs(seed, part) draws one part's arguments, and reference() takes and returns one part's arrays. A program takes and returns all parts, laid end to end along the dimension named above; an argument that names none is the same for every part. Nothing has to cross between parts.
Inputs may be any that keep to these rules, and one draw needn't show every extreme that they name: reset_points[b] lies in the b-th of 8 equal spans of the sequence and is never that span's first position.
All inputs are finite; a program needn't handle non-finite values.
Results may differ from the reference program's by a relative error of at most 0.0058.
Values may be sent and summed in bfloat16 or wider, within the bound.
No kernel may reach another device: no remote copies, remote signals or barrier semaphores. Data moves between devices by JAX's collectives and lax.ppermute only.
A program may use at most 384 MiB of HBM per device.

```python
import jax
import jax.numpy as jnp
from jax import lax

HD = 128
HEADS = 8
D = 2048
TOK_DEV = 384
TOKENS = 6144
RESETS = 8
N_CTX = 16


def draw_reset_points(key, part):
    key = jax.random.fold_in(key, 11)
    span = TOKENS // RESETS
    offsets = jax.random.randint(key, (RESETS,), 1, span, dtype=jnp.int32)
    return (jnp.arange(RESETS, dtype=jnp.int32) * span + offsets).astype(jnp.int32)


def levels(key, shape, split, smallest, largest):
    factor_of = 1.0
    for axis_at, shards_of in split:
        steps = jax.random.uniform(jax.random.fold_in(jax.random.fold_in(key, 6), axis_at), (shards_of,), jnp.float32, smallest / len(split), largest / len(split))
        factor_of = factor_of * jnp.repeat(jnp.exp(steps), shape[axis_at] // shards_of).reshape((-1,) + (1,) * (len(shape) - 1 - axis_at))
    return factor_of


def normal_values(own_key, shape, deviation, most, split=(), kind=jnp.bfloat16):
    factor_of = levels(own_key, shape, split, -0.22, 0.18) if split else 1.0
    drawn = jax.random.normal(own_key, shape, jnp.float32) * deviation * factor_of
    return jnp.minimum(jnp.maximum(drawn, -most), most).astype(kind)


def setup_inputs(seed: int = 0, part: int = 0) -> dict:
    seeds = jax.random.split(jax.random.key(seed), 7)
    part_splits = jax.random.split(jax.random.fold_in(seeds[6], part), 7)
    queries = normal_values(part_splits[0], (TOKENS, HEADS * HD), 1.0, 6.0, ((0, 16),))
    keys = normal_values(part_splits[1], (TOKENS, HEADS * HD), 1.0, 6.0, ((0, 16),))
    values = normal_values(part_splits[2], (TOKENS, HEADS * HD), 1.0, 6.0, ((0, 16),))
    reset_points = draw_reset_points(jax.random.fold_in(jax.random.fold_in(seeds[6], part), 71), part)
    norm_gain = jnp.clip(1.0 + 0.18 * jax.random.normal(seeds[4], (HEADS * HD,), jnp.float32), 0.1, 1.9)
    out_weight = normal_values(seeds[5], (HEADS * HD, D), (HEADS * HD) ** -0.5, 0.1875, ((1, 16),))
    return {"queries": queries, "keys": keys, "values": values, "reset_points": reset_points, "norm_gain": norm_gain, "out_weight": out_weight}


HIGH = lax.Precision.HIGHEST
EPS = 1e-05

def reference(queries, keys, values, reset_points, norm_gain, out_weight):
    head_count = HEADS
    positions = jnp.arange(TOKENS, dtype=jnp.int32)
    segment = lax.optimization_barrier(jnp.sum((positions[:, None] >= reset_points[None, :]).astype(jnp.int32), axis=1))
    query_blocks = queries.reshape(N_CTX, TOK_DEV, head_count, HD)
    key_blocks = keys.reshape(N_CTX, TOK_DEV, head_count, HD)
    value_blocks = values.reshape(N_CTX, TOK_DEV, head_count, HD)
    seg_blocks = segment.reshape(N_CTX, TOK_DEV)
    stretch_ids = jnp.arange(N_CTX, dtype=jnp.int32)
    offsets = jnp.arange(TOK_DEV, dtype=jnp.int32)
    causal = offsets[None, :] <= offsets[:, None]
    later_mask = offsets[None, :] > offsets[:, None]
    gain_heads = norm_gain.reshape(head_count, HD)

    def step(carry, inputs):
        key_prev, val_prev, pair_prev = carry
        q_blk, k_blk, v_blk, seg_blk, stretch_id = inputs
        query_heads = q_blk.astype(jnp.float32)
        key_heads = k_blk.astype(jnp.float32)
        value_heads = v_blk.astype(jnp.float32)
        first_pos = stretch_id * TOK_DEV
        seg_before = jnp.sum((reset_points < first_pos).astype(jnp.int32))
        same_seg = seg_blk[:, None] == seg_blk[None, :]
        visible = causal & same_seg
        rounded = jnp.einsum('thd,ihd->hti', query_heads, key_heads).astype(jnp.bfloat16)
        lower = jnp.where(visible[None], rounded, jnp.zeros((), jnp.bfloat16)).astype(jnp.float32)
        pair_scores = jnp.einsum('hti,hji->htj', lower, lower)
        pair_scores = jnp.where(visible[None], pair_scores, jnp.float32(0.0)).astype(jnp.bfloat16)
        inside = jnp.einsum('htj,jhd->thd', pair_scores.astype(jnp.float32), value_heads)
        tail_rows = seg_blk == seg_blk[-1]
        key_tail = jnp.where(tail_rows[:, None, None], key_heads, jnp.float32(0.0))
        query_tail = jnp.where(tail_rows[:, None, None], query_heads, jnp.float32(0.0))
        key_cov = jnp.einsum('ihd,ihe->hde', key_tail, key_heads)
        val_cov = jnp.einsum('jhd,jhe->hde', query_tail, value_heads)
        upper = jnp.where((later_mask & same_seg)[None], rounded, jnp.zeros((), jnp.bfloat16)).astype(jnp.float32)
        carried = jnp.einsum('hji,jhd->ihd', upper, value_heads).astype(jnp.bfloat16)
        pair_sum = jnp.einsum('ihd,ihe->hde', key_tail, carried.astype(jnp.float32))
        reset_flag = seg_blk[-1] != seg_before
        history = jnp.einsum('hij,hjk->hik', key_prev, val_prev, precision=HIGH) - pair_prev
        open_rows = seg_blk == seg_before
        q_state = jnp.einsum('thd,hde->hte', query_heads, key_prev, precision=HIGH).astype(jnp.bfloat16)
        reach = causal & open_rows[:, None]
        mixed_scores = jnp.einsum('hte,jhe->htj', q_state.astype(jnp.float32), query_heads)
        mixed_scores = jnp.where(reach[None], mixed_scores, jnp.float32(0.0)).astype(jnp.bfloat16)
        across = jnp.einsum('htj,jhd->thd', mixed_scores.astype(jnp.float32), value_heads)
        across = across + jnp.einsum('thd,hde->the', query_heads, history, precision=HIGH)
        across = jnp.where(open_rows[:, None, None], across, jnp.float32(0.0))
        summed = inside + across
        inverse = lax.rsqrt(lax.optimization_barrier(jnp.mean(summed * summed, axis=2, keepdims=True)) + EPS)
        hidden = (summed * inverse * gain_heads[None]).astype(jnp.bfloat16).reshape(TOK_DEV, head_count * HD)
        block_out = jnp.dot(hidden, out_weight, preferred_element_type=jnp.float32).astype(jnp.bfloat16)
        through = jnp.einsum('hij,hjk->hik', key_cov, val_prev, precision=HIGH)
        new_key = jnp.where(reset_flag, key_cov, key_prev + key_cov)
        new_val = jnp.where(reset_flag, val_cov, val_prev + val_cov)
        new_pair = jnp.where(reset_flag, pair_sum, pair_prev + pair_sum + through)
        return ((new_key, new_val, new_pair), block_out)
    zeros = jnp.zeros((head_count, HD, HD), jnp.float32)
    unused, outputs = lax.scan(step, (zeros, zeros, zeros), (query_blocks, key_blocks, value_blocks, seg_blocks, stretch_ids))
    return outputs.reshape(TOKENS, D)
```

```python
import functools

import jax
import jax.numpy as jnp
from jax import lax
from jax.experimental import pallas as pl
from jax.experimental.pallas import tpu as pltpu
from jax.sharding import PartitionSpec as P

HD = 128
EPS = 1e-05
BF = jnp.bfloat16
F32 = jnp.float32
VMEM_LIMIT = 48 * 1024 * 1024


def dot(a, b, ca, cb):
    return lax.dot_general(a, b, (((ca,), (cb,)), ((), ())), preferred_element_type=F32)


def params(**more):
    return pltpu.CompilerParams(vmem_limit_bytes=VMEM_LIMIT, **more)


def visible_mask(cut, length):
    row = lax.broadcasted_iota(jnp.int32, (length, length), 0)
    col = lax.broadcasted_iota(jnp.int32, (length, length), 1)
    return (col <= row) & ((row < cut) | (col >= cut))


def state_kernel(heads, info, q_ref, k_ref, v_ref, w_ref, st_ref):
    length = q_ref.shape[0]
    cut, has = info[0], info[1]
    visible = visible_mask(cut, length)
    row = lax.broadcasted_iota(jnp.int32, (length, HD), 0)
    tail = (row >= cut) | (has == 0)
    zero = jnp.zeros((), BF)
    for h in range(heads):
        at = slice(h * HD, (h + 1) * HD)
        q, k, v = q_ref[:, at], k_ref[:, at], v_ref[:, at]
        scores = jnp.where(visible, dot(q, k, 1, 1), 0.0).astype(BF)
        w = dot(scores, k, 1, 0).astype(BF)
        w_ref[:, at] = w
        v_tail = jnp.where(tail, v, zero)
        k_tail = jnp.where(tail, k, zero)
        st_ref[0, h] = dot(k_tail, k, 0, 0).astype(BF)
        st_ref[1, h] = dot(q, v_tail, 0, 0).astype(BF)
        st_ref[2, h] = dot(w, v_tail, 0, 0).astype(BF)


def chip_kernel(half, info, own_ref, other_ref, out_ref):
    core, has_second = info[2], info[3]
    first = core == 0
    for j in range(half):
        h = core * half + j
        own = [own_ref[n, h].astype(F32) for n in range(3)]
        oth = [other_ref[n, h].astype(F32) for n in range(3)]
        s0, h0 = jnp.where(first, own[0], oth[0]), jnp.where(first, own[2], oth[2])
        s1, c1, h1 = (jnp.where(first, oth[n], own[n]) for n in range(3))
        through = dot(s0.astype(BF), c1.astype(BF), 1, 0)
        keep = has_second == 0
        out_ref[0, j] = jnp.where(keep, s0 + s1, s1).astype(BF)
        out_ref[1, j] = jnp.where(keep, h0 + h1 + through, h1).astype(BF)


def output_kernel(heads, half, info, q_ref, v_ref, w_ref, gain_ref, other_ref, same_ref, swap_ref, out_ref):
    length = q_ref.shape[0]
    cut, has, core, keep_chip = info[0], info[1], info[2], info[4]
    visible = visible_mask(cut, length)
    row = lax.broadcasted_iota(jnp.int32, (length, HD), 0)
    is_open = (row < cut) | (has == 0)
    step = pl.program_id(0)
    for h in range(heads):
        at = slice(h * HD, (h + 1) * HD)
        head = step * heads + h
        place = lax.rem(head, half)
        mine = lax.div(head, half) == core
        s_chip = jnp.where(mine, same_ref[0, place], swap_ref[0, place]).astype(F32)
        h_chip = jnp.where(mine, same_ref[1, place], swap_ref[1, place]).astype(F32)
        s_chip = jnp.where(keep_chip == 1, s_chip, 0.0)
        h_chip = jnp.where(keep_chip == 1, h_chip, 0.0)
        s_in, c_in, h_in = (other_ref[n, h].astype(F32) for n in range(3))
        through = dot(s_chip.astype(BF), c_in.astype(BF), 1, 0)
        second = core == 1
        s_prev = jnp.where(second, s_chip + s_in, s_chip).astype(BF)
        h_prev = jnp.where(second, h_chip + h_in + through, h_chip).astype(BF)
        q, v = q_ref[:, at], v_ref[:, at]
        w = w_ref[:, at].astype(F32) + jnp.where(is_open, dot(q, s_prev, 1, 0), 0.0)
        scores = jnp.where(visible, dot(q, w.astype(BF), 1, 1), 0.0).astype(BF)
        summed = dot(scores, v, 1, 0) + jnp.where(is_open, dot(q, h_prev, 1, 0), 0.0)
        inverse = lax.rsqrt(jnp.mean(summed * summed, axis=1, keepdims=True) + EPS)
        out_ref[:, at] = (summed * inverse * gain_ref[:, at]).astype(BF)


def project_kernel(pairs, info, hidden_ref, *refs):
    same, other, out_ref = refs[:pairs], refs[pairs : 2 * pairs], refs[-1]
    first = info[2] == 0
    for n in range(pairs):
        cols = same[n].shape[1]
        a, b = same[n][...], other[n][...]
        both = jnp.concatenate([jnp.where(first, a, b), jnp.where(first, b, a)], axis=1)
        at = pl.multiple_of(info[8 + n], 2 * cols)
        out_ref[:, pl.ds(at, 2 * cols)] = dot(hidden_ref[...], both, 1, 0).astype(BF)


def smem():
    return pl.BlockSpec(memory_space=pltpu.SMEM)


def swap_by(mask, n):
    return [(i, i ^ mask) for i in range(n)]


def on_device(blocks, queries, keys, values, reset_points, norm_gain, out_weight):
    length, width = queries.shape
    heads = width // HD
    half = heads // 2
    n_ctx = blocks
    per_span = n_ctx // reset_points.shape[0]
    assert per_span == 2 and heads % 2 == 0
    index = lax.axis_index("ctx")
    core, chip = index % 2, index // 2
    local = reset_points[chip] - index * length
    has = (local >= 0) & (local < length)
    local_pair = reset_points[chip] - chip * 2 * length
    has_second = local_pair >= length
    cut = jnp.where(has, local, 0)
    keep_chip = (chip > 0) & ((core == 0) | has_second)
    masks = [0, 2, 4, 6, 8, 10, 12, 14]
    info = jnp.stack(
        [cut, has, core, has_second, keep_chip, cut, cut, cut]
        + [((index ^ m) // 2) * 2 * out_weight.shape[1] for m in masks]
    ).astype(jnp.int32)

    small = n_ctx == 16 and out_weight.shape[1] == HD
    if small:
        x_swap = functools.partial(lax.ppermute, axis_name="ctx", perm=swap_by(2, n_ctx))
        z_got = {m: lax.ppermute(out_weight, "ctx", swap_by(m, n_ctx)) for m in (4, 8, 12)}
        pieces = {0: out_weight, 2: x_swap(out_weight)}
        for m in (4, 8, 12):
            pieces[m] = z_got[m]
            pieces[m + 2] = x_swap(z_got[m])
        same = [pieces[m] for m in masks]
        other = [lax.ppermute(p, "ctx", swap_by(1, n_ctx)) for p in same]

    step_heads = 2
    steps = heads // step_heads
    block = step_heads * HD
    row_spec = pl.BlockSpec((length, block), lambda s: (0, s))
    state_spec = pl.BlockSpec((3, step_heads, HD, HD), lambda s: (0, s, 0, 0))
    w, state = pl.pallas_call(
        functools.partial(state_kernel, step_heads),
        grid=(steps,),
        in_specs=[smem(), row_spec, row_spec, row_spec],
        out_specs=[row_spec, state_spec],
        out_shape=[
            jax.ShapeDtypeStruct((length, width), BF),
            jax.ShapeDtypeStruct((3, heads, HD, HD), BF),
        ],
        compiler_params=params(),
        name="block_state",
    )(info, queries, keys, values)
    state_other = lax.ppermute(state, "ctx", swap_by(1, n_ctx))
    chip_state = pl.pallas_call(
        functools.partial(chip_kernel, half),
        in_specs=[smem(), pl.BlockSpec(memory_space=pltpu.VMEM), pl.BlockSpec(memory_space=pltpu.VMEM)],
        out_shape=jax.ShapeDtypeStruct((2, half, HD, HD), BF),
        compiler_params=params(),
        name="chip_state",
    )(info, state, state_other)
    before = lax.ppermute(chip_state, "ctx", [(i, i + 2) for i in range(n_ctx - 2)])
    before_swap = lax.ppermute(before, "ctx", swap_by(1, n_ctx))
    hidden = pl.pallas_call(
        functools.partial(output_kernel, step_heads, half),
        grid=(steps,),
        in_specs=[
            smem(),
            row_spec,
            row_spec,
            row_spec,
            pl.BlockSpec((1, block), lambda s: (0, s)),
            state_spec,
            pl.BlockSpec((2, half, HD, HD), lambda s: (0, 0, 0, 0)),
            pl.BlockSpec((2, half, HD, HD), lambda s: (0, 0, 0, 0)),
        ],
        out_specs=row_spec,
        out_shape=jax.ShapeDtypeStruct((length, width), BF),
        compiler_params=params(),
        name="block_output",
    )(info, queries, values, w, norm_gain.reshape(1, width), state_other, before, before_swap)
    if not small:
        whole = lax.all_gather(out_weight, "ctx", axis=1, tiled=True)
        return jnp.dot(hidden, whole, preferred_element_type=F32).astype(BF)
    pairs = len(masks)
    return pl.pallas_call(
        functools.partial(project_kernel, pairs),
        in_specs=[smem()] + [pl.BlockSpec(memory_space=pltpu.VMEM)] * (1 + 2 * pairs),
        out_shape=jax.ShapeDtypeStruct((length, n_ctx * out_weight.shape[1]), BF),
        compiler_params=params(),
        name="project",
    )(info, hidden, *same, *other)


def solution(mesh):
    placed = (
        P(("groups", "ctx"), None),
        P(("groups", "ctx"), None),
        P(("groups", "ctx"), None),
        P("groups"),
        P(),
        P(None, "ctx"),
    )
    return jax.shard_map(
        functools.partial(on_device, mesh.shape["ctx"]),
        mesh=mesh,
        in_specs=placed,
        out_specs=P(("groups", "ctx"), None),
        check_vma=False,
    )
```

```python
import functools

import jax
import jax.numpy as jnp
from jax import lax
from jax.experimental import pallas as pl
from jax.experimental.pallas import tpu as pltpu
from jax.sharding import PartitionSpec as P

HD = 128
EPS = 1e-05
BF = jnp.bfloat16
F32 = jnp.float32
MIB = 1024 * 1024


def dot(a, b, ca, cb):
    return lax.dot_general(a, b, (((ca,), (cb,)), ((), ())), preferred_element_type=F32)


def params(mib=48):
    return pltpu.CompilerParams(vmem_limit_bytes=mib * MIB)


def scalars(resets, blocks, length):
    index = lax.axis_index("ctx")
    core, chip = lax.rem(index, 2), lax.div(index, 2)
    pair = resets[chip] - chip * (2 * length)
    local = pair - core * length
    has = (local >= 0) & (local < length)
    cut = jnp.where(has, local, 0)
    has_second = pair >= length
    return index, core, chip, has, cut, has_second


def visible_mask(cut, length):
    row = lax.broadcasted_iota(jnp.int32, (length, length), 0)
    col = lax.broadcasted_iota(jnp.int32, (length, length), 1)
    return (col <= row) & ((row < cut) | (col >= cut))


def state_kernel(blocks, heads, step, resets, q_hbm, k_hbm, v_hbm, w_ref, *refs):
    steps = heads // step
    st_refs, (q_ref, k_ref, v_ref, sems) = refs[:steps], refs[steps:]
    length = q_ref.shape[0]
    width = step * HD
    copies = []
    for s in range(steps):
        at = slice(s * width, (s + 1) * width)
        for n, (src, dst) in enumerate(((q_hbm, q_ref), (k_hbm, k_ref), (v_hbm, v_ref))):
            copy = pltpu.make_async_copy(src.at[:, at], dst.at[:, at], sems.at[n, s])
            copy.start()
            copies.append(copy)
    _, _, _, has, cut, _ = scalars(resets, blocks, length)
    visible = visible_mask(cut, length)
    row = lax.broadcasted_iota(jnp.int32, (length, HD), 0)
    tail = (row >= cut) | jnp.logical_not(has)
    zero = jnp.zeros((), BF)
    for h in range(heads):
        if h % step == 0:
            for n in range(3):
                copies[(h // step) * 3 + n].wait()
        at = slice(h * HD, (h + 1) * HD)
        q, k, v = q_ref[:, at], k_ref[:, at], v_ref[:, at]
        scores = jnp.where(visible, dot(q, k, 1, 1), 0.0).astype(BF)
        w = dot(scores, k, 1, 0).astype(BF)
        w_ref[:, at] = w
        v_tail = jnp.where(tail, v, zero)
        k_tail = jnp.where(tail, k, zero)
        st_refs[h // step][0, h % step] = dot(k_tail, k, 0, 0).astype(BF)
        st_refs[h // step][1, h % step] = dot(q, v_tail, 0, 0).astype(BF)
        st_refs[h // step][2, h % step] = dot(w, v_tail, 0, 0).astype(BF)


def chip_kernel(blocks, length, half, step, resets, *refs):
    _, core, _, _, _, has_second = scalars(resets, blocks, length)
    groups = 2 * half // step
    own_refs, other_refs, out_ref = refs[:groups], refs[groups : 2 * groups], refs[-2:]
    first = core == 0
    keep = jnp.logical_not(has_second)
    for j in range(half):
        low, high = j // step, (j + half) // step

        def part(refs, n):
            return jnp.where(first, refs[low][n, j % step], refs[high][n, j % step]).astype(F32)

        own = [part(own_refs, n) for n in range(3)]
        oth = [part(other_refs, n) for n in range(3)]
        s0, h0 = jnp.where(first, own[0], oth[0]), jnp.where(first, own[2], oth[2])
        s1, c1, h1 = (jnp.where(first, oth[n], own[n]) for n in range(3))
        through = dot(s0.astype(BF), c1.astype(BF), 1, 0)
        out_ref[0][j] = jnp.where(keep, s0 + s1, s1).astype(BF)
        out_ref[1][j] = jnp.where(keep, h0 + h1 + through, h1).astype(BF)


def output_kernel(blocks, heads, half, resets, q_ref, v_ref, w_ref, gain_ref, *refs):
    same_ref, swap_ref, other_refs, out_ref = refs[:2], refs[2:4], refs[4:-1], refs[-1]
    step = heads // len(other_refs)
    length = q_ref.shape[0]
    _, core, chip, has, cut, has_second = scalars(resets, blocks, length)
    second = core == 1
    keep_chip = (chip > 0) & (jnp.logical_not(second) | has_second)
    visible = visible_mask(cut, length)
    row = lax.broadcasted_iota(jnp.int32, (length, HD), 0)
    is_open = (row < cut) | jnp.logical_not(has)
    for h in range(heads):
        at = slice(h * HD, (h + 1) * HD)
        place = h % half
        mine = core == h // half
        s_chip = jnp.where(mine, same_ref[0][place], swap_ref[0][place]).astype(F32)
        h_chip = jnp.where(mine, same_ref[1][place], swap_ref[1][place]).astype(F32)
        s_chip = jnp.where(keep_chip, s_chip, 0.0)
        h_chip = jnp.where(keep_chip, h_chip, 0.0)
        s_in, c_in, h_in = (other_refs[h // step][n, h % step].astype(F32) for n in range(3))
        through = dot(s_chip.astype(BF), c_in.astype(BF), 1, 0)
        s_prev = jnp.where(second, s_chip + s_in, s_chip).astype(BF)
        h_prev = jnp.where(second, h_chip + h_in + through, h_chip).astype(BF)
        q, v = q_ref[:, at], v_ref[:, at]
        w = w_ref[:, at].astype(F32) + jnp.where(is_open, dot(q, s_prev, 1, 0), 0.0)
        scores = jnp.where(visible, dot(q, w.astype(BF), 1, 1), 0.0).astype(BF)
        summed = dot(scores, v, 1, 0) + jnp.where(is_open, dot(q, h_prev, 1, 0), 0.0)
        inverse = lax.rsqrt(jnp.mean(summed * summed, axis=1, keepdims=True) + EPS)
        out_ref[:, at] = (summed * inverse * gain_ref[:, at]).astype(BF)


def project_kernel(masks, hidden_ref, *refs):
    pairs = len(masks)
    same, other, (out_hbm, buffer, sems) = refs[:pairs], refs[pairs : 2 * pairs], refs[-3:]
    index = lax.axis_index("ctx")
    first = lax.rem(index, 2) == 0
    cols = 2 * same[0].shape[1]
    copies = []
    for n, mask in enumerate(masks):
        a, b = same[n][...], other[n][...]
        both = jnp.concatenate([jnp.where(first, a, b), jnp.where(first, b, a)], axis=1)
        buffer[n] = dot(hidden_ref[...], both, 1, 0).astype(BF)
        at = pl.multiple_of(lax.div(index ^ mask, 2) * cols, cols)
        copy = pltpu.make_async_copy(buffer.at[n], out_hbm.at[:, pl.ds(at, cols)], sems.at[n])
        copy.start()
        copies.append(copy)
    for copy in copies:
        copy.wait()


def project(hidden, masks, same, other, shape, before=None):
    pairs = len(masks)
    extra = [] if before is None else [before]
    length, cols = hidden.shape[0], 2 * same[0].shape[1]
    return pl.pallas_call(
        functools.partial(project_kernel, masks),
        in_specs=[pl.BlockSpec(memory_space=pltpu.VMEM)] * (1 + 2 * pairs) + [anywhere()] * len(extra),
        out_specs=anywhere(),
        out_shape=shape,
        input_output_aliases={} if before is None else {1 + 2 * pairs: 0},
        scratch_shapes=[pltpu.VMEM((pairs, length, cols), BF), pltpu.SemaphoreType.DMA((pairs,))],
        compiler_params=params(),
        name="project",
    )(hidden, *same, *other, *extra)


def anywhere():
    return pl.BlockSpec(memory_space=pltpu.HBM)


def smem():
    return pl.BlockSpec(memory_space=pltpu.SMEM)


def swap_by(mask, n):
    return [(i, i ^ mask) for i in range(n)]


def on_device(blocks, queries, keys, values, reset_points, norm_gain, out_weight):
    length, width = queries.shape
    heads = width // HD
    half = heads // 2
    n_ctx = blocks
    per_span = n_ctx // reset_points.shape[0]
    assert per_span == 2 and heads % 2 == 0
    small = n_ctx == 16 and out_weight.shape[1] == HD

    def swap(piece, mask, *after):
        if after:
            piece, *_ = lax.optimization_barrier((piece, *after))
        return lax.ppermute(piece, "ctx", swap_by(mask, n_ctx))

    if small:
        pieces = {0: out_weight, 2: swap(out_weight, 2), 4: swap(out_weight, 4), 8: swap(out_weight, 8)}

    step_heads = 2
    steps = heads // step_heads
    whole_vmem = pl.BlockSpec(memory_space=pltpu.VMEM)
    any_place = pl.BlockSpec(memory_space=pl.ANY)
    w, *state = pl.pallas_call(
        functools.partial(state_kernel, n_ctx, heads, step_heads),
        in_specs=[smem(), anywhere(), anywhere(), anywhere()],
        out_specs=[whole_vmem] * (1 + steps),
        out_shape=[jax.ShapeDtypeStruct((length, width), BF)]
        + [jax.ShapeDtypeStruct((3, step_heads, HD, HD), BF)] * steps,
        scratch_shapes=[pltpu.VMEM((length, width), BF)] * 3 + [pltpu.SemaphoreType.DMA((3, steps))],
        compiler_params=params(),
        name="block_state",
    )(reset_points, *(pltpu.with_memory_space_constraint(a, pltpu.HBM) for a in (queries, keys, values)))
    if small:
        *state_sent, _, _ = lax.optimization_barrier((*state, pieces[2], pieces[4]))
    else:
        state_sent = state
    state_other = [swap(part, 1) for part in state_sent]
    waited = []
    if small:
        pieces[6] = swap(pieces[4], 2, w)
        waited = [pieces[6], pieces[8]]
    chip_state = pl.pallas_call(
        functools.partial(chip_kernel, n_ctx, length, half, step_heads),
        in_specs=[smem()] + [whole_vmem] * (2 * steps) + [any_place] * len(waited),
        out_shape=[jax.ShapeDtypeStruct((half, HD, HD), BF)] * 2,
        compiler_params=params(),
        name="chip_state",
    )(reset_points, *state, *state_other, *waited)
    before = [lax.ppermute(part, "ctx", [(i, i + 2) for i in range(n_ctx - 2)]) for part in chip_state]
    if small:
        pieces[12] = swap(out_weight, 12, pieces[4])
        for m in (8, 12):
            pieces[m + 2] = swap(pieces[m], 2)
        others = {m: swap(pieces[m], 1) for m in (0, 2, 4, 6, 8, 10, 12)}
        before_swap = [swap(part, 1, pieces[12], pieces[10]) for part in before]
    else:
        before_swap = [swap(part, 1) for part in before]
    hidden = pl.pallas_call(
        functools.partial(output_kernel, n_ctx, heads, half),
        in_specs=[smem()] + [whole_vmem] * (8 + steps),
        out_shape=jax.ShapeDtypeStruct((length, width), BF),
        compiler_params=params(),
        name="block_output",
    )(reset_points, queries, values, w, norm_gain.reshape(1, width), *before, *before_swap, *state_other)
    if not small:
        whole = lax.all_gather(out_weight, "ctx", axis=1, tiled=True)
        return jnp.dot(hidden, whole, preferred_element_type=F32).astype(BF)
    shape = jax.ShapeDtypeStruct((length, n_ctx * out_weight.shape[1]), BF)
    masks = (0, 2, 4, 6, 8, 10, 12)
    out = project(hidden, masks, [pieces[m] for m in masks], [others[m] for m in masks], shape)
    last = swap(pieces[14], 1, out)
    return project(hidden, (14,), [pieces[14]], [last], shape, out)


def solution(mesh):
    placed = (
        P(("groups", "ctx"), None),
        P(("groups", "ctx"), None),
        P(("groups", "ctx"), None),
        P("groups"),
        P(),
        P(None, "ctx"),
    )
    return jax.shard_map(
        functools.partial(on_device, mesh.shape["ctx"]),
        mesh=mesh,
        in_specs=placed,
        out_specs=P(("groups", "ctx"), None),
        check_vma=False,
    )
```

```python
import functools

import jax
import jax.numpy as jnp
from jax import lax
from jax.experimental import pallas as pl
from jax.experimental.pallas import tpu as pltpu
from jax.sharding import PartitionSpec as P

HD = 128
EPS = 1e-05
BF = jnp.bfloat16
F32 = jnp.float32
MIB = 1024 * 1024


def dot(a, b, ca, cb):
    return lax.dot_general(a, b, (((ca,), (cb,)), ((), ())), preferred_element_type=F32)


def params(mib=48):
    return pltpu.CompilerParams(vmem_limit_bytes=mib * MIB)


def scalars(resets, blocks, length):
    index = lax.axis_index("ctx")
    core, chip = lax.rem(index, 2), lax.div(index, 2)
    pair = resets[chip] - chip * (2 * length)
    local = pair - core * length
    has = (local >= 0) & (local < length)
    cut = jnp.where(has, local, 0)
    has_second = pair >= length
    return index, core, chip, has, cut, has_second


def visible_mask(cut, length):
    row = lax.broadcasted_iota(jnp.int32, (length, length), 0)
    col = lax.broadcasted_iota(jnp.int32, (length, length), 1)
    return (col <= row) & ((row < cut) | (col >= cut))


def state_kernel(blocks, heads, step, resets, q_hbm, k_hbm, v_hbm, w_ref, *refs):
    steps = heads // step
    st_refs, (q_ref, k_ref, v_ref, sems) = refs[:steps], refs[steps:]
    length = q_ref.shape[0]
    width = step * HD
    copies = []
    for s in range(steps):
        at = slice(s * width, (s + 1) * width)
        for n, (src, dst) in enumerate(((q_hbm, q_ref), (k_hbm, k_ref), (v_hbm, v_ref))):
            copy = pltpu.make_async_copy(src.at[:, at], dst.at[:, at], sems.at[n, s])
            copy.start()
            copies.append(copy)
    _, _, _, has, cut, _ = scalars(resets, blocks, length)
    visible = jnp.where(visible_mask(cut, length), 1.0, 0.0).astype(BF)
    row = lax.broadcasted_iota(jnp.int32, (length, HD), 0)
    tail = jnp.where((row >= cut) | jnp.logical_not(has), 1.0, 0.0).astype(BF)

    def score(h):
        at = slice(h * HD, (h + 1) * HD)
        return dot(q_ref[:, at], k_ref[:, at], 1, 1).astype(BF) * visible

    def finish(h, scores):
        at = slice(h * HD, (h + 1) * HD)
        q, k, v = q_ref[:, at], k_ref[:, at], v_ref[:, at]
        w = dot(scores, k, 1, 0).astype(BF)
        w_ref[:, at] = w
        out = st_refs[h // step]
        out[0, h % step] = dot((k * tail).T, k, 1, 0).astype(BF)
        both = dot((v * tail).T, jnp.concatenate([q, w], axis=1), 1, 0).astype(BF)
        out[1, h % step] = both[:, :HD]
        out[2, h % step] = both[:, HD:]

    ahead = None
    for h in range(heads):
        if h % step == 0:
            for n in range(3):
                copies[(h // step) * 3 + n].wait()
        scores = score(h)
        if h > 0:
            finish(h - 1, ahead)
        ahead = scores
    finish(heads - 1, ahead)


def chip_kernel(blocks, length, half, step, resets, *refs):
    _, core, _, _, _, has_second = scalars(resets, blocks, length)
    groups = 2 * half // step
    own_refs, other_refs, out_ref = refs[:groups], refs[groups : 2 * groups], refs[-1]
    first = core == 0
    keep = jnp.logical_not(has_second)
    for j in range(half):
        low, high = j // step, (j + half) // step

        def part(refs, n):
            return jnp.where(first, refs[low][n, j % step], refs[high][n, j % step]).astype(F32)

        own = [part(own_refs, n) for n in range(3)]
        oth = [part(other_refs, n) for n in range(3)]
        s0, h0 = jnp.where(first, own[0], oth[0]), jnp.where(first, own[2], oth[2])
        s1, c1, h1 = (jnp.where(first, oth[n], own[n]) for n in range(3))
        through = dot(c1.astype(BF), s0.astype(BF), 1, 1)
        out_ref[0, j] = jnp.where(keep, s0 + s1, s1).astype(BF)
        out_ref[1, j] = jnp.where(keep, h0 + h1 + through, h1).astype(BF)


def output_kernel(blocks, heads, half, resets, q_ref, v_ref, w_ref, gain_ref, *refs):
    same_ref, swap_ref, other_refs, out_ref = refs[0], refs[1], refs[2:-1], refs[-1]
    step = heads // len(other_refs)
    length = q_ref.shape[0]
    _, core, chip, has, cut, has_second = scalars(resets, blocks, length)
    second = core == 1
    keep_chip = (chip > 0) & (jnp.logical_not(second) | has_second)
    visible = visible_mask(cut, length)
    row = lax.broadcasted_iota(jnp.int32, (length, HD), 0)
    is_open = (row < cut) | jnp.logical_not(has)
    for h in range(heads):
        at = slice(h * HD, (h + 1) * HD)
        place = h % half
        mine = core == h // half
        s_chip = jnp.where(mine, same_ref[0, place], swap_ref[0, place]).astype(F32)
        h_chip = jnp.where(mine, same_ref[1, place], swap_ref[1, place]).astype(F32)
        s_chip = jnp.where(keep_chip, s_chip, 0.0)
        h_chip = jnp.where(keep_chip, h_chip, 0.0)
        s_in, c_in, h_in = (other_refs[h // step][n, h % step].astype(F32) for n in range(3))
        through = dot(c_in.astype(BF), s_chip.astype(BF), 1, 1)
        s_prev = jnp.where(second, s_chip + s_in, s_chip).astype(BF)
        h_prev = jnp.where(second, h_chip + h_in + through, h_chip).astype(BF)
        q, v = q_ref[:, at], v_ref[:, at]
        w = w_ref[:, at].astype(F32) + jnp.where(is_open, dot(q, s_prev, 1, 0), 0.0)
        scores = jnp.where(visible, dot(q, w.astype(BF), 1, 1), 0.0).astype(BF)
        summed = dot(scores, v, 1, 0) + jnp.where(is_open, dot(q, h_prev, 1, 1), 0.0)
        inverse = lax.rsqrt(jnp.mean(summed * summed, axis=1, keepdims=True) + EPS)
        out_ref[:, at] = (summed * inverse * gain_ref[:, at]).astype(BF)


def project_kernel(masks, hidden_ref, *refs):
    pairs = len(masks)
    same, other, (out_hbm, buffer, sems) = refs[:pairs], refs[pairs : 2 * pairs], refs[-3:]
    index, group = lax.axis_index("ctx"), lax.axis_index("groups")
    first = lax.rem(index, 2) == 0
    cols = 2 * same[0].shape[1]
    copies = []
    for n, mask in enumerate(masks):
        a, b = same[n][...], other[n][...]
        both = jnp.concatenate([jnp.where(first, a, b), jnp.where(first, b, a)], axis=1)
        buffer[n] = dot(hidden_ref[...], both, 1, 0).astype(BF)
        place = index ^ jnp.where(group == 0, mask[0], mask[1])
        at = pl.multiple_of(lax.div(place, 2) * cols, cols)
        copy = pltpu.make_async_copy(buffer.at[n], out_hbm.at[:, pl.ds(at, cols)], sems.at[n])
        copy.start()
        copies.append(copy)
    for copy in copies:
        copy.wait()


def project(hidden, masks, same, other, shape, before=None):
    pairs = len(masks)
    extra = [] if before is None else [before]
    length, cols = hidden.shape[0], 2 * same[0].shape[1]
    return pl.pallas_call(
        functools.partial(project_kernel, masks),
        in_specs=[pl.BlockSpec(memory_space=pltpu.VMEM)] * (1 + 2 * pairs) + [anywhere()] * len(extra),
        out_specs=anywhere(),
        out_shape=shape,
        input_output_aliases={} if before is None else {1 + 2 * pairs: 0},
        scratch_shapes=[pltpu.VMEM((pairs, length, cols), BF), pltpu.SemaphoreType.DMA((pairs,))],
        compiler_params=params(),
        name="project",
    )(hidden, *same, *other, *extra)


def anywhere():
    return pl.BlockSpec(memory_space=pltpu.HBM)


def smem():
    return pl.BlockSpec(memory_space=pltpu.SMEM)


def swap_by(mask, n):
    return [(i, i ^ mask) for i in range(n)]


def on_device(groups, blocks, queries, keys, values, reset_points, norm_gain, out_weight):
    length, width = queries.shape
    heads = width // HD
    half = heads // 2
    n_ctx = blocks
    per_span = n_ctx // reset_points.shape[0]
    assert per_span == 2 and heads % 2 == 0
    small = n_ctx == 16 and groups == 2 and out_weight.shape[1] == HD

    def after(piece, *done):
        return lax.optimization_barrier((piece, *done))[0] if done else piece

    def swap(piece, mask, *done):
        return lax.ppermute(after(piece, *done), "ctx", swap_by(mask, n_ctx))

    def swap_groups(piece, *done):
        return lax.ppermute(after(piece, *done), "groups", [(0, 1), (1, 0)])

    if small:
        far = [(g * n_ctx + i, g * n_ctx + (i ^ mask)) for g, mask in enumerate((8, 12)) for i in range(n_ctx)]
        pieces = {
            (0, 0): out_weight,
            (2, 2): swap(out_weight, 2),
            (4, 4): swap(out_weight, 4),
            (8, 12): lax.ppermute(out_weight, ("groups", "ctx"), far),
        }

    step_heads = 2
    steps = heads // step_heads
    whole_vmem = pl.BlockSpec(memory_space=pltpu.VMEM)
    any_place = pl.BlockSpec(memory_space=pl.ANY)
    w, *state = pl.pallas_call(
        functools.partial(state_kernel, n_ctx, heads, step_heads),
        in_specs=[smem(), anywhere(), anywhere(), anywhere()],
        out_specs=[whole_vmem] * (1 + steps),
        out_shape=[jax.ShapeDtypeStruct((length, width), BF)]
        + [jax.ShapeDtypeStruct((3, step_heads, HD, HD), BF)] * steps,
        scratch_shapes=[pltpu.VMEM((length, width), BF)] * 3 + [pltpu.SemaphoreType.DMA((3, steps))],
        compiler_params=params(),
        name="block_state",
    )(reset_points, *(pltpu.with_memory_space_constraint(a, pltpu.HBM) for a in (queries, keys, values)))
    if small:
        *state_sent, _, _ = lax.optimization_barrier((*state, pieces[2, 2], pieces[4, 4]))
    else:
        state_sent = state
    state_other = [swap(part, 1) for part in state_sent]
    if small:
        pieces[6, 6] = swap(pieces[4, 4], 2, w)
    waited = [pieces[8, 12], pieces[6, 6]] if small else []
    chip_state = pl.pallas_call(
        functools.partial(chip_kernel, n_ctx, length, half, step_heads),
        in_specs=[smem()] + [whole_vmem] * (2 * steps) + [any_place] * len(waited),
        out_shape=jax.ShapeDtypeStruct((2, half, HD, HD), BF),
        compiler_params=params(),
        name="chip_state",
    )(reset_points, *state, *state_other, *waited)
    before = lax.ppermute(chip_state, "ctx", [(i, i + 2) for i in range(n_ctx - 2)])
    if small:
        pieces[10, 14] = swap(pieces[8, 12], 2)
        pieces[12, 8] = swap_groups(pieces[8, 12])
        pieces[14, 10] = swap_groups(pieces[10, 14])
        others = {m: swap(pieces[m], 1) for m in pieces if m != (14, 10)}
        before_swap = swap(before, 1, pieces[12, 8], pieces[10, 14])
    else:
        before_swap = swap(before, 1)
    hidden = pl.pallas_call(
        functools.partial(output_kernel, n_ctx, heads, half),
        in_specs=[smem()] + [whole_vmem] * (6 + steps),
        out_shape=jax.ShapeDtypeStruct((length, width), BF),
        compiler_params=params(),
        name="block_output",
    )(reset_points, queries, values, w, norm_gain.reshape(1, width), before, before_swap, *state_other)
    if not small:
        whole = lax.all_gather(out_weight, "ctx", axis=1, tiled=True)
        return jnp.dot(hidden, whole, preferred_element_type=F32).astype(BF)
    shape = jax.ShapeDtypeStruct((length, n_ctx * out_weight.shape[1]), BF)
    masks = tuple(others)
    out = project(hidden, masks, [pieces[m] for m in masks], [others[m] for m in masks], shape)
    last = swap(pieces[14, 10], 1, out)
    return project(hidden, ((14, 10),), [pieces[14, 10]], [last], shape, out)


def solution(mesh):
    placed = (
        P(("groups", "ctx"), None),
        P(("groups", "ctx"), None),
        P(("groups", "ctx"), None),
        P("groups"),
        P(),
        P(None, "ctx"),
    )
    return jax.shard_map(
        functools.partial(on_device, mesh.shape["groups"], mesh.shape["ctx"]),
        mesh=mesh,
        in_specs=placed,
        out_specs=P(("groups", "ctx"), None),
        check_vma=False,
    )
```
